512 devices in a mesh: win: 16 (over x, z_hi, core), tile: 32 (over z_lo, y).
Axes of the slice: x: 4, y: 8, z: 8 (z_hi: 2, z_lo: 4; z = z_hi * 4 + z_lo), core: 2. Of those that a mesh axis runs over, the one named last changes fastest.
Arguments:
- increment: float32 [16, 128, 256, 512], P('win', None, 'tile'), may hold values from -6 to 6
- diffusivity: float32 [16, 256, 512], P('win', 'tile'), may hold values from 0.04 to 0.2
- wind: float32 [16, 128], P('win'), may hold values from -0.3 to 0.3
- vertical_cov: bfloat16 [128, 128], replicated, may hold values from -1 to 2, as said below
- row_cov: bfloat16 [256, 256], replicated, may hold values from -1 to 2, as said below
- column_cov: bfloat16 [512, 512], replicated, may hold values from -1 to 2, as said below
Outputs:
- covaried: float32 [16, 128, 256, 512], P('win', 'tile')
The draws below stay inside these ranges and needn't reach their ends.
Inputs may be any that keep to these rules, and one draw needn't show every extreme that they name: `vertical_cov`: symmetric and positive definite. `row_cov`: symmetric and positive definite. `column_cov`: symmetric and positive definite.
All inputs are finite; a program needn't handle non-finite values.
Results may differ from the reference program's by a relative error of at most 0.0003.
Values sent between devices are 32-bit elements; how exact they have to be, the bound alone decides.
A program may use at most 64 MiB of HBM per device.

```python
import jax
import jax.numpy as jnp
from jax import lax

L = 128
NY = 256
NX = 512
STEPS = 6
WIN = 16


def covariance(key, count):
    factor = jax.random.normal(key, (count, count), jnp.float32)
    product = jnp.dot(factor, factor.T, precision=jax.lax.Precision.HIGHEST) / count
    return 0.6 * jnp.eye(count, dtype=jnp.float32) + 0.4 * product


def draw_vertical_cov(key, part):
    return covariance(jax.random.fold_in(key, 11), L).astype(jnp.bfloat16)


def draw_row_cov(key, part):
    return covariance(jax.random.fold_in(key, 23), NY).astype(jnp.bfloat16)


def draw_column_cov(key, part):
    return covariance(jax.random.fold_in(key, 37), NX).astype(jnp.bfloat16)


def block_levels(stream_key, extent, shards, least, high):
    def one(position, parts):
        draws = jax.random.uniform(jax.random.fold_in(jax.random.fold_in(stream_key, 6), position), (parts,), jnp.float32, least / len(shards), high / len(shards))
        return jnp.repeat(jnp.exp(draws), extent[position] // parts).reshape((-1,) + (1,) * (len(extent) - position - 1))

    gain = one(*shards[0])
    for cut in shards[1:]:
        gain = gain * one(*cut)
    return gain


def normal_values(own_key, extent, scale, bound, shards=(), kind=jnp.bfloat16):
    array = jax.random.normal(own_key, extent, jnp.float32) * scale
    if len(shards) > 0:
        array = block_levels(own_key, extent, shards, -0.22, 0.18) * array
    return jnp.clip(array, min=-bound, max=bound).astype(kind)


def setup_inputs(seed: int = 0) -> dict:
    seeds = jax.random.split(jax.random.key(seed), 7)
    return {
        "increment": normal_values(seeds[0], (WIN, L, NY, NX), 1.0, 6.0, ((0, 16), (2, 32)), jnp.float32),
        "diffusivity": jnp.clip(0.04 + 0.16 * jax.random.uniform(seeds[1], (WIN, NY, NX), jnp.float32) ** block_levels(seeds[1], (WIN, NY, NX), ((0, 16), (1, 32)), -0.2, 0.2), 0.04, 0.2),
        "wind": jnp.clip(jax.random.uniform(seeds[2], (WIN, L), jnp.float32, -0.3, 0.3) * block_levels(seeds[2], (WIN, L), ((0, 16),), -0.4, 0.0), -0.3, 0.3),
        "vertical_cov": draw_vertical_cov(jax.random.fold_in(seeds[6], 71), 0),
        "row_cov": draw_row_cov(jax.random.fold_in(seeds[6], 71), 0),
        "column_cov": draw_column_cov(jax.random.fold_in(seeds[6], 71), 0),
    }


VMIX = 0.1


def tendency(center, north, south, kappa, wind_col):
    east = jnp.roll(center, -1, axis=2)
    west = jnp.roll(center, 1, axis=2)
    stacked = jnp.pad(center, ((1, 1), (0, 0), (0, 0)))
    upper = stacked[2:]
    lower = stacked[:-2]
    horiz = north + south + east + west - 4.0 * center
    vert = upper + lower - 2.0 * center
    return center + kappa[None] * horiz + VMIX * vert + wind_col * (0.5 * (south - north))


def reference(increment, diffusivity, wind, vertical_cov, row_cov, column_cov):
    vert_mat = vertical_cov.astype(jnp.float32)
    row_mat = row_cov.astype(jnp.float32)
    col_mat = column_cov.astype(jnp.float32)
    last = increment.shape[0] - 1

    def one(index):
        field = lax.dynamic_index_in_dim(increment, index, 0, keepdims=False)
        kappa = lax.dynamic_index_in_dim(diffusivity, index, 0, keepdims=False)
        wind_col = lax.dynamic_index_in_dim(wind, index, 0, keepdims=False)[:, None, None]
        later = jnp.minimum(index + 1, last).astype(jnp.int32)
        following = lax.dynamic_index_in_dim(increment, later, 0, keepdims=False)
        following = jnp.where(index < last, following, jnp.zeros_like(following))
        current = field
        for step in range(STEPS):
            padded = jnp.pad(current, ((0, 0), (1, 1), (0, 0)))
            current = tendency(current, padded[:, 2:], padded[:, :-2], kappa, wind_col)
        defect = current - following
        levels, height, width = defect.shape
        mixed = jnp.dot(vert_mat, defect.reshape(levels, height * width), precision=lax.Precision.HIGHEST)
        mixed = jnp.dot(mixed.reshape(levels * height, width), col_mat, precision=lax.Precision.HIGHEST)
        mixed = mixed.reshape(levels, height, width)
        return jnp.einsum("yk,zkx->zyx", row_mat, mixed, precision=lax.Precision.HIGHEST)

    return lax.map(one, jnp.arange(increment.shape[0], dtype=jnp.int32))
```

```python
import functools

import jax
import jax.numpy as jnp
from jax import lax
from jax.experimental import pallas as pl
from jax.experimental.pallas import tpu as pltpu
from jax.sharding import PartitionSpec as P

STEPS = 6
L, ROWS, NX = 128, 8, 512
NY = 256
C = NX // 128
H = STEPS
R20 = ROWS + 2 * H
PAD = 8
MESH = pl.DeviceIdType.MESH
F32, BF16 = jnp.float32, jnp.bfloat16


def split2(v):
    hi = v.astype(BF16)
    lo = (v - hi.astype(F32)).astype(BF16)
    return hi, lo


def kernel(
    inc_ref, dif_ref, wind_ref, vert_ref, row_ref, col_ref, out_ref,
    inb, x, xb, kap, wbuf, fb, mf, me, ze, zf, g, rb, zb, ob,
    in_sem, dif_sem, out_sem, loc_e, loc_y,
    halo_s, halo_r, kap_s, kap_r, raw_s, raw_r, f_s, f_r, e_s, e_r, y_s, y_r, go_sem,
):
    w = lax.axis_index("win")
    tile = lax.axis_index("tile")
    core = lax.rem(w, 2)
    a = tile // 8
    yy = lax.rem(tile, 8)
    even, odd = core == 0, core == 1
    has_prev, has_next = tile > 0, tile < 31
    sends_f = jnp.logical_and(even, w > 0)
    gets_f = jnp.logical_and(odd, w < 15)

    in_cps = [
        pltpu.make_async_copy(inc_ref.at[:, pl.ds(128 * c, 128)], inb.at[c], in_sem.at[c])
        for c in range(C)
    ]
    for cp in in_cps:
        cp.start()
    dif_cps = [
        pltpu.make_async_copy(dif_ref.at[:, pl.ds(128 * c, 128)], kap.at[1, c], dif_sem.at[c])
        for c in range(C)
    ]
    for cp in dif_cps:
        cp.start()

    bar = pltpu.get_barrier_semaphore()

    def greet(dev):
        pl.semaphore_signal(bar, inc=1, device_id=dev, device_id_type=MESH)

    pl.when(has_prev)(lambda: greet((w, tile - 1)))
    pl.when(has_next)(lambda: greet((w, tile + 1)))
    for d in range(1, 4):
        greet((w, lax.rem(a + d, 4) * 8 + yy))
    for d in range(1, 8):
        greet((w, a * 8 + lax.rem(yy + d, 8)))
    sib = w + 1 - 2 * core
    greet((sib, tile))

    @pl.when(gets_f)
    def _():
        for b in range(4):
            greet((w + 1, b * 8 + yy))

    zero8 = jnp.zeros((8, 128), F32)

    @pl.loop(0, R20)
    def _(r):
        for f in (x, xb):
            for c in range(C):
                f[c, r, 0:8, :] = zero8
                f[c, r, PAD + L : PAD + L + 8, :] = zero8

    def clear_rows(first):
        @pl.loop(first, first + H)
        def _(r):
            for f in (x, xb):
                for c in range(C):
                    f[c, r, PAD : PAD + L, :] = jnp.zeros((L, 128), F32)

    pl.when(jnp.logical_not(has_prev))(lambda: clear_rows(0))
    pl.when(jnp.logical_not(has_next))(lambda: clear_rows(H + ROWS))

    wbuf[...] = jnp.transpose(jnp.broadcast_to(wind_ref[...] * 5.0, (128, 128)))
    vert = vert_ref[...]
    vv = jnp.concatenate([vert, vert], axis=1)

    for cp in in_cps:
        cp.wait()
    for c in range(C):
        for y in range(ROWS):
            x[c, H + y, PAD : PAD + L, :] = inb[c, pl.ds(y, L, stride=8), :]
    for cp in dif_cps:
        cp.wait()

    peers = 11 + has_prev.astype(jnp.int32) + has_next.astype(jnp.int32) + jnp.where(sends_f, 4, 0)
    pl.semaphore_wait(bar, peers)

    raw = pltpu.make_async_remote_copy(
        src_ref=inb, dst_ref=fb, send_sem=raw_s, recv_sem=raw_r,
        device_id=(sib, tile), device_id_type=MESH,
    )

    @pl.when(odd)
    def _():
        raw.start()
        pl.semaphore_wait(go_sem, 1)

    def remote(src, dst, ss, rs, dev):
        return pltpu.make_async_remote_copy(
            src_ref=src, dst_ref=dst, send_sem=ss, recv_sem=rs, device_id=dev, device_id_type=MESH
        )

    zs = pl.ds(PAD, L)
    up = remote(
        x.at[:, pl.ds(H, H), zs], x.at[:, pl.ds(H + ROWS, H), zs],
        halo_s.at[0], halo_r.at[0], (w, tile - 1),
    )
    down = remote(
        x.at[:, pl.ds(ROWS, H), zs], x.at[:, pl.ds(0, H), zs],
        halo_s.at[1], halo_r.at[1], (w, tile + 1),
    )
    kup = remote(kap.at[1], kap.at[2], kap_s.at[0], kap_r.at[0], (w, tile - 1))
    kdown = remote(kap.at[1], kap.at[0], kap_s.at[1], kap_r.at[1], (w, tile + 1))

    @pl.when(has_prev)
    def _():
        kup.start()
        up.start()

    @pl.when(has_next)
    def _():
        kdown.start()
        down.start()

    def level_mix(fields, c, dst, scale=None, base=None):
        @pl.loop(0, ROWS // 2)
        def _(pair):
            parts = []
            for i in range(2):
                y = 2 * pair + i
                v = fields[c, H + y, PAD : PAD + L, :]
                if scale is not None:
                    v = v * scale - base[c, pl.ds(y, L, stride=8), :]
                parts.append(v)
            hi, lo = split2(jnp.concatenate(parts, axis=1))
            mixed = jnp.dot(vv, jnp.concatenate([hi, lo], axis=0), preferred_element_type=F32)
            for i in range(2):
                for b in range(4):
                    dst[b, c, 2 * pair + i] = mixed[32 * b : 32 * b + 32, 128 * i : 128 * i + 128]

    f_cps = [
        remote(
            mf.at[lax.rem(a + d, 4)], zf.at[a], f_s.at[d], f_r.at[d],
            (lax.rem(w + 15, 16), lax.rem(a + d, 4) * 8 + yy),
        )
        for d in range(4)
    ]

    @pl.when(sends_f)
    def _():
        for c in range(C):
            level_mix(x, c, mf)
        for cp in f_cps:
            cp.start()

    @pl.when(jnp.logical_not(gets_f))
    def _():
        @pl.loop(0, 4)
        def _(i):
            for c in range(C):
                zf[i, c] = jnp.zeros((ROWS, 32, 128), F32)

    @pl.when(odd)
    def _():
        @pl.loop(0, C)
        def _(c):
            fb[c] = jnp.zeros((L * ROWS, 128), F32)

    @pl.when(has_prev)
    def _():
        kup.wait_send()
        kdown.wait_recv()
        down.wait_recv()

    @pl.when(has_next)
    def _():
        kdown.wait_send()
        kup.wait_recv()
        up.wait_recv()

    @pl.when(even)
    def _():
        pl.semaphore_signal(go_sem, inc=1, device_id=(sib, tile), device_id_type=MESH)

    pl.when(has_prev)(lambda: up.wait_send())
    pl.when(has_next)(lambda: down.wait_send())

    lane = lax.broadcasted_iota(jnp.int32, (8, 128), 1)
    first_lane, last_lane = lane == 0, lane == 127
    low = jnp.where(has_prev, 0, H)
    high = jnp.where(has_next, R20, H + ROWS)

    def step(s, src, dst):
        @pl.loop(jnp.maximum(low, s + 1), jnp.minimum(high, R20 - 1 - s))
        def _(r):
            kr = r + 2
            kt, ks = kr // 8, lax.rem(kr, 8)
            kb = [jnp.broadcast_to(kap[kt, c, pl.ds(ks, 1), :] * 10.0, (8, 128)) for c in range(C)]
            ab = [8.0 - 4.0 * k for k in kb]
            for zt in range(L // 8):
                z0 = PAD + 8 * zt
                wz = wbuf[8 * zt : 8 * zt + 8, :]
                cs = [src[c, r, z0 : z0 + 8, :] for c in range(C)]
                rr = [pltpu.roll(v, 1, 1) for v in cs]
                rl = [pltpu.roll(v, 127, 1) for v in cs]
                for c in range(C):
                    west = jnp.where(first_lane, rr[(c + C - 1) % C], rr[c])
                    east = jnp.where(last_lane, rl[(c + 1) % C], rl[c])
                    north = src[c, r + 1, z0 : z0 + 8, :]
                    south = src[c, r - 1, z0 : z0 + 8, :]
                    vert_sum = src[c, r, z0 + 1 : z0 + 9, :] + src[c, r, z0 - 1 : z0 + 7, :]
                    dst[c, r, z0 : z0 + 8, :] = (
                        (vert_sum + ab[c] * cs[c])
                        + kb[c] * ((north + south) + (east + west))
                        + wz * (south - north)
                    )

    @pl.loop(0, STEPS // 2)
    def _(h):
        step(2 * h, x, xb)
        step(2 * h + 1, xb, x)

    pl.when(even)(lambda: raw.wait_recv())

    e_cps = [[None] * 4 for _ in range(C)]
    e_loc = []
    for c in range(C):
        level_mix(x, c, me, 1e-6, fb)
        for d in (1, 3, 2):
            b = lax.rem(a + d, 4)
            cp = remote(me.at[b, c], ze.at[a, c], e_s.at[c, d], e_r.at[c, d], (w, b * 8 + yy))
            cp.start()
            e_cps[c][d] = cp
        cp = pltpu.make_async_copy(me.at[a, c], ze.at[a, c], loc_e.at[c])
        cp.start()
        e_loc.append(cp)

    @pl.when(gets_f)
    def _():
        for cp in f_cps:
            cp.wait_recv()

    y_cps = [[None] * 8 for _ in range(C)]
    y_loc = []
    for c in range(C):
        for d in (1, 3, 2):
            e_cps[c][d].wait_recv()
        e_loc[c].wait()

        @pl.loop(0, 4)
        def _(i, c=c):
            for y in range(ROWS):
                for t in range(4):
                    v = ze[i, c, y, 8 * t : 8 * t + 8, :] - zf[i, c, y, 8 * t : 8 * t + 8, :]
                    at = pl.ds(pl.multiple_of(i * 32, 32) + 4 * y, 4)
                    g[c, 2 * t, at, :] = v[0:4]
                    g[c, 2 * t + 1, at, :] = v[4:8]

        for d in (1, 7, 2, 6, 3, 5, 4):
            t = lax.rem(yy + d, 8)
            cp = remote(g.at[c, t], rb.at[yy, c], y_s.at[c, d], y_r.at[c, d], (w, a * 8 + t))
            cp.start()
            y_cps[c][d] = cp
        cp = pltpu.make_async_copy(g.at[c, yy], rb.at[yy, c], loc_y.at[c])
        cp.start()
        y_loc.append(cp)

    for d in (0, 1, 7, 2, 6, 3, 5, 4):
        src = lax.rem(yy + 8 - d, 8)
        for c in range(C):
            if d == 0:
                y_loc[c].wait()
            else:
                y_cps[c][d].wait_recv()
        total = None
        for c in range(C):
            v = jnp.concatenate([rb[src, c, pl.ds(z, 32, stride=4), :] for z in range(4)], axis=0)
            hi, lo = split2(v)
            cm = col_ref[128 * c : 128 * c + 128, :]
            part = jnp.dot(hi, cm, preferred_element_type=F32) + jnp.dot(lo, cm, preferred_element_type=F32)
            total = part if total is None else total + part
        for z in range(4):
            for i in range(4):
                k = z * 32 + i * 8
                zb[z, pl.ds(pl.multiple_of(64 * i + 8 * src, 8), 8), :] = total[k : k + 8]

    outs = []
    for z in range(4):
        hi, lo = split2(zb[z])
        rm = row_ref[...]
        ob[z] = jnp.dot(rm, hi, preferred_element_type=F32) + jnp.dot(rm, lo, preferred_element_type=F32)
        cp = pltpu.make_async_copy(ob.at[z], out_ref.at[z], out_sem.at[z])
        cp.start()
        outs.append(cp)

    pl.when(odd)(lambda: raw.wait_send())

    @pl.when(sends_f)
    def _():
        for cp in f_cps:
            cp.wait_send()

    for c in range(C):
        for d in range(1, 4):
            e_cps[c][d].wait_send()
        for d in range(1, 8):
            y_cps[c][d].wait_send()
    for cp in outs:
        cp.wait()


def body(increment, diffusivity, wind, vertical_cov, row_cov, column_cov):
    dma = pltpu.SemaphoreType.DMA
    anyspec = pl.BlockSpec(memory_space=pl.ANY)
    vm = pl.BlockSpec(memory_space=pltpu.VMEM)
    out = pl.pallas_call(
        kernel,
        out_shape=jax.ShapeDtypeStruct((4, NY, NX), F32),
        in_specs=[anyspec, anyspec, vm, vm, vm, vm],
        out_specs=anyspec,
        scratch_shapes=[
            pltpu.VMEM((C, L * ROWS, 128), F32),
            pltpu.VMEM((C, R20, L + 2 * PAD, 128), F32),
            pltpu.VMEM((C, R20, L + 2 * PAD, 128), F32),
            pltpu.VMEM((3, C, ROWS, 128), F32),
            pltpu.VMEM((L, 128), F32),
            pltpu.VMEM((C, L * ROWS, 128), F32),
            pltpu.VMEM((4, C, ROWS, 32, 128), F32),
            pltpu.VMEM((4, C, ROWS, 32, 128), F32),
            pltpu.VMEM((4, C, ROWS, 32, 128), F32),
            pltpu.VMEM((4, C, ROWS, 32, 128), F32),
            pltpu.VMEM((C, 8, 128, 128), F32),
            pltpu.VMEM((8, C, 128, 128), F32),
            pltpu.VMEM((4, NY, NX), F32),
            pltpu.VMEM((4, NY, NX), F32),
            dma((C,)), dma((C,)), dma((4,)), dma((C,)), dma((C,)),
            dma((2,)), dma((2,)), dma((2,)), dma((2,)), dma, dma,
            dma((4,)), dma((4,)), dma((C, 4)), dma((C, 4)), dma((C, 8)), dma((C, 8)),
            pltpu.SemaphoreType.REGULAR,
        ],
        compiler_params=pltpu.CompilerParams(
            collective_id=0, has_side_effects=True, vmem_limit_bytes=56 * 1024 * 1024
        ),
    )(
        increment.reshape(L * ROWS, NX), diffusivity[0], wind, vertical_cov, row_cov, column_cov
    )
    return out[None]


def solution(mesh):
    in_specs = (P("win", None, "tile", None), P("win", "tile", None), P("win", None), P(), P(), P())
    out_specs = P("win", "tile", None, None)
    return jax.shard_map(body, mesh=mesh, in_specs=in_specs, out_specs=out_specs, check_vma=False)
```

```python
import functools

import jax
import jax.numpy as jnp
from jax import lax
from jax.experimental import pallas as pl
from jax.experimental.pallas import tpu as pltpu
from jax.sharding import PartitionSpec as P

STEPS = 6
L, ROWS, NX = 128, 8, 512
NY = 256
C = NX // 128
H = STEPS
R20 = ROWS + 2 * H
PAD = 8
AHEAD = 2
ORDER = [dz * 8 + dy for dy in (4, 3, 5, 2, 6, 1, 7, 0) for dz in (2, 1, 3, 0) if dz or dy]
MESH = pl.DeviceIdType.MESH
F32, BF16 = jnp.float32, jnp.bfloat16


def split2(v):
    hi = v.astype(BF16)
    lo = (v - hi.astype(F32)).astype(BF16)
    return hi, lo


def kernel(
    inc_ref, dif_ref, wind_ref, vert_ref, row_ref, col_ref, out_ref,
    inb, x, xb, kap, wbuf, fb, mf, me, md, ze, zf, g, rb, zb, ob,
    in_sem, dif_sem, out_sem, loc_e, loc_y, loc_d,
    halo_s, halo_r, kap_s, kap_r, raw_s, raw_r, f_s, f_r, e_s, e_r, y_s, y_r, d_s, d_r, go_sem,
):
    w = lax.axis_index("win")
    tile = lax.axis_index("tile")
    core = lax.rem(w, 2)
    a = tile // 8
    yy = lax.rem(tile, 8)
    even, odd = core == 0, core == 1
    has_prev, has_next = tile > 0, tile < 31
    sends_f = jnp.logical_and(even, w > 0)
    gets_f = jnp.logical_and(odd, w < 15)

    in_cps = [
        pltpu.make_async_copy(inc_ref.at[:, pl.ds(128 * c, 128)], inb.at[c], in_sem.at[c])
        for c in range(C)
    ]
    for cp in in_cps:
        cp.start()
    dif_cps = [
        pltpu.make_async_copy(dif_ref.at[:, pl.ds(128 * c, 128)], kap.at[1, c], dif_sem.at[c])
        for c in range(C)
    ]
    for cp in dif_cps:
        cp.start()

    bar = pltpu.get_barrier_semaphore()

    def greet(dev):
        pl.semaphore_signal(bar, inc=1, device_id=dev, device_id_type=MESH)

    pl.when(has_prev)(lambda: greet((w, tile - 1)))
    pl.when(has_next)(lambda: greet((w, tile + 1)))

    @pl.when(even)
    def _():
        @pl.loop(1, 32)
        def _(d):
            greet((w, lax.rem(tile + d, 32)))

    @pl.when(odd)
    def _():
        for d in range(1, 4):
            greet((w, lax.rem(a + d, 4) * 8 + yy))
        for d in range(1, 8):
            greet((w, a * 8 + lax.rem(yy + d, 8)))

    sib = w + 1 - 2 * core
    greet((sib, tile))

    @pl.when(gets_f)
    def _():
        for b in range(4):
            greet((w + 1, b * 8 + yy))

    zero8 = jnp.zeros((8, 128), F32)

    @pl.loop(0, R20)
    def _(r):
        for f in (x, xb):
            for c in range(C):
                f[c, r, 0:8, :] = zero8
                f[c, r, PAD + L : PAD + L + 8, :] = zero8

    def clear_rows(first):
        @pl.loop(first, first + H)
        def _(r):
            for f in (x, xb):
                for c in range(C):
                    f[c, r, PAD : PAD + L, :] = jnp.zeros((L, 128), F32)

    pl.when(jnp.logical_not(has_prev))(lambda: clear_rows(0))
    pl.when(jnp.logical_not(has_next))(lambda: clear_rows(H + ROWS))

    wbuf[...] = jnp.transpose(jnp.broadcast_to(wind_ref[...] * 5.0, (128, 128)))
    vert = vert_ref[...]
    vv = jnp.concatenate([vert, vert], axis=1)

    for cp in in_cps:
        cp.wait()
    for c in range(C):
        for y in range(ROWS):
            x[c, H + y, PAD : PAD + L, :] = inb[c, pl.ds(y, L, stride=8), :]
    for cp in dif_cps:
        cp.wait()

    def level_mix(fields, c, dst, scale=None, base=None):
        @pl.loop(0, ROWS // 2)
        def _(pair):
            parts = []
            for i in range(2):
                y = 2 * pair + i
                v = fields[c, H + y, PAD : PAD + L, :]
                if scale is not None:
                    v = v * scale
                if base is not None:
                    v = v - base[c, pl.ds(y, L, stride=8), :]
                parts.append(v)
            hi, lo = split2(jnp.concatenate(parts, axis=1))
            mixed = jnp.dot(vv, jnp.concatenate([hi, lo], axis=0), preferred_element_type=F32)
            for i in range(2):
                if dst is md:
                    at = pl.ds(pl.multiple_of(8 * pair, 8) + 4 * i, 4)
                    for t in range(32):
                        dst[t, c, at, :] = mixed[4 * t : 4 * t + 4, 128 * i : 128 * i + 128]
                    continue
                for b in range(4):
                    dst[b, c, 2 * pair + i] = mixed[32 * b : 32 * b + 32, 128 * i : 128 * i + 128]

    @pl.when(sends_f)
    def _():
        for c in range(C):
            level_mix(x, c, mf)

    peers = jnp.where(even, 32, 11) + has_prev.astype(jnp.int32) + has_next.astype(jnp.int32) + jnp.where(sends_f, 4, 0)
    pl.semaphore_wait(bar, peers)

    def remote(src, dst, ss, rs, dev):
        return pltpu.make_async_remote_copy(
            src_ref=src, dst_ref=dst, send_sem=ss, recv_sem=rs, device_id=dev, device_id_type=MESH
        )

    raw = pltpu.make_async_remote_copy(
        src_ref=inb, dst_ref=fb, send_sem=raw_s, recv_sem=raw_r,
        device_id=(sib, tile), device_id_type=MESH,
    )

    pl.when(odd)(lambda: raw.start())

    f_cps = [
        [
            remote(
                mf.at[lax.rem(a + d, 4), c], zf.at[a, c], f_s.at[c, d], f_r.at[c, d],
                (lax.rem(w + 15, 16), lax.rem(a + d, 4) * 8 + yy),
            )
            for d in range(4)
        ]
        for c in range(C)
    ]

    edge = jnp.logical_or(yy == 0, yy == 7)

    @pl.when(jnp.logical_and(sends_f, jnp.logical_not(edge)))
    def _():
        for cps in f_cps:
            for cp in cps:
                cp.start()

    @pl.when(even)
    def _():
        pl.semaphore_wait(go_sem, 1)


    zs = pl.ds(PAD, L)
    up = remote(
        x.at[:, pl.ds(H, H), zs], x.at[:, pl.ds(H + ROWS, H), zs],
        halo_s.at[0], halo_r.at[0], (w, tile - 1),
    )
    down = remote(
        x.at[:, pl.ds(ROWS, H), zs], x.at[:, pl.ds(0, H), zs],
        halo_s.at[1], halo_r.at[1], (w, tile + 1),
    )
    kup = remote(kap.at[1], kap.at[2], kap_s.at[0], kap_r.at[0], (w, tile - 1))
    kdown = remote(kap.at[1], kap.at[0], kap_s.at[1], kap_r.at[1], (w, tile + 1))

    @pl.when(jnp.logical_and(sends_f, edge))
    def _():
        for cps in f_cps:
            for cp in cps:
                cp.start()

    @pl.when(has_prev)
    def _():
        kup.start()
        up.start()

    @pl.when(has_next)
    def _():
        kdown.start()
        down.start()

    @pl.when(w == 15)
    def _():
        @pl.loop(0, 4)
        def _(i):
            for c in range(C):
                zf[i, c] = jnp.zeros((ROWS, 32, 128), F32)

    @pl.when(has_prev)
    def _():
        kup.wait_send()
        kdown.wait_recv()
        down.wait_recv()

    @pl.when(has_next)
    def _():
        kdown.wait_send()
        kup.wait_recv()
        up.wait_recv()

    @pl.when(jnp.logical_not(even))
    def _():
        pl.semaphore_signal(go_sem, inc=1, device_id=(sib, tile), device_id_type=MESH)

    pl.when(has_prev)(lambda: up.wait_send())
    pl.when(has_next)(lambda: down.wait_send())

    lane = lax.broadcasted_iota(jnp.int32, (8, 128), 1)
    first_lane, last_lane = lane == 0, lane == 127
    low = jnp.where(has_prev, 0, H)
    high = jnp.where(has_next, R20, H + ROWS)

    def step(s, src, dst):
        @pl.loop(jnp.maximum(low, s + 1), jnp.minimum(high, R20 - 1 - s))
        def _(r):
            kr = r + 2
            kt, ks = kr // 8, lax.rem(kr, 8)
            kb = [jnp.broadcast_to(kap[kt, c, pl.ds(ks, 1), :] * 10.0, (8, 128)) for c in range(C)]
            ab = [8.0 - 4.0 * k for k in kb]
            for zt in range(L // 8):
                z0 = PAD + 8 * zt
                wz = wbuf[8 * zt : 8 * zt + 8, :]
                cs = [src[c, r, z0 : z0 + 8, :] for c in range(C)]
                rr = [pltpu.roll(v, 1, 1) for v in cs]
                rl = [pltpu.roll(v, 127, 1) for v in cs]
                for c in range(C):
                    west = jnp.where(first_lane, rr[(c + C - 1) % C], rr[c])
                    east = jnp.where(last_lane, rl[(c + 1) % C], rl[c])
                    north = src[c, r + 1, z0 : z0 + 8, :]
                    south = src[c, r - 1, z0 : z0 + 8, :]
                    vert_sum = src[c, r, z0 + 1 : z0 + 9, :] + src[c, r, z0 - 1 : z0 + 7, :]
                    dst[c, r, z0 : z0 + 8, :] = (
                        (vert_sum + ab[c] * cs[c])
                        + kb[c] * ((north + south) + (east + west))
                        + wz * (south - north)
                    )

    @pl.loop(0, STEPS // 2)
    def _(h):
        step(2 * h, x, xb)
        step(2 * h + 1, xb, x)

    d_cps = {}
    for d in ORDER:
        dz, dy = d // 8, d % 8
        t = lax.rem(a + dz, 4) * 8 + lax.rem(yy + dy, 8)
        d_cps[d] = remote(
            md.at[t], rb.at[yy, :, pl.ds(pl.multiple_of(32 * a, 32), 32)], d_s.at[d], d_r.at[d], (w, t)
        )
    d_loc = pltpu.make_async_copy(md.at[tile], rb.at[yy, :, pl.ds(pl.multiple_of(32 * a, 32), 32)], loc_d)

    @pl.when(even)
    def _():
        raw.wait_recv()
        for c in range(C):
            level_mix(x, c, md, 1e-6, fb)
        for d in ORDER:
            d_cps[d].start()
        d_loc.start()
        d_loc.wait()

    e_cps = [[None] * 4 for _ in range(C)]
    e_loc = []
    y_cps = [[None] * 8 for _ in range(C)]
    y_loc = []
    for c in range(C):
        for d in (1, 3, 2):
            b = lax.rem(a + d, 4)
            e_cps[c][d] = remote(me.at[b, c], ze.at[a, c], e_s.at[c, d], e_r.at[c, d], (w, b * 8 + yy))
        e_loc.append(pltpu.make_async_copy(me.at[a, c], ze.at[a, c], loc_e.at[c]))
        for d in (1, 7, 2, 6, 3, 5, 4):
            t = lax.rem(yy + d, 8)
            y_cps[c][d] = remote(g.at[c, t], rb.at[yy, c], y_s.at[c, d], y_r.at[c, d], (w, a * 8 + t))
        y_loc.append(pltpu.make_async_copy(g.at[c, yy], rb.at[yy, c], loc_y.at[c]))

    def send_levels(c):
        level_mix(x, c, me, 1e-6)
        if c >= AHEAD:
            for d in (1, 3, 2):
                e_cps[c - AHEAD][d].wait_recv()
        for d in (1, 3, 2):
            e_cps[c][d].start()
        e_loc[c].start()

    def send_rows(c):
        @pl.loop(0, 4)
        def _(i):
            for y in range(ROWS):
                for t in range(4):
                    v = ze[i, c, y, 8 * t : 8 * t + 8, :] - zf[i, c, y, 8 * t : 8 * t + 8, :]
                    at = pl.ds(pl.multiple_of(i * 32, 32) + 4 * y, 4)
                    g[c, 2 * t, at, :] = v[0:4]
                    g[c, 2 * t + 1, at, :] = v[4:8]

        for d in (4, 3, 5, 2, 6, 1, 7):
            y_cps[c][d].start()
        y_loc[c].start()

    @pl.when(odd)
    def _():
        for c in range(AHEAD):
            send_levels(c)
        for c in range(C):
            if c + AHEAD < C:
                send_levels(c + AHEAD)
            else:
                for d in (1, 3, 2):
                    e_cps[c][d].wait_recv()
            e_loc[c].wait()

            @pl.when(gets_f)
            def _(c=c):
                for cp in f_cps[c]:
                    cp.wait_recv()

            send_rows(c)
        for c in range(C):
            y_loc[c].wait()

    for d in (0, 4, 3, 5, 2, 6, 1, 7):
        src = lax.rem(yy + 8 - d, 8)

        @pl.when(even)
        def _(d=d):
            for dz in range(4):
                if dz or d:
                    d_cps[dz * 8 + d].wait_recv()

        if d:

            @pl.when(odd)
            def _(d=d):
                for c in range(C):
                    y_cps[c][d].wait_recv()

        total = None
        for c in range(C):
            v = jnp.concatenate([rb[src, c, pl.ds(z, 32, stride=4), :] for z in range(4)], axis=0)
            hi, lo = split2(v)
            cm = col_ref[128 * c : 128 * c + 128, :]
            part = jnp.dot(hi, cm, preferred_element_type=F32) + jnp.dot(lo, cm, preferred_element_type=F32)
            total = part if total is None else total + part
        for z in range(4):
            for i in range(4):
                k = z * 32 + i * 8
                zb[z, pl.ds(pl.multiple_of(64 * i + 8 * src, 8), 8), :] = total[k : k + 8]

    outs = []
    for z in range(4):
        hi, lo = split2(zb[z])
        rm = row_ref[...]
        ob[z] = jnp.dot(rm, hi, preferred_element_type=F32) + jnp.dot(rm, lo, preferred_element_type=F32)
        cp = pltpu.make_async_copy(ob.at[z], out_ref.at[z], out_sem.at[z])
        cp.start()
        outs.append(cp)

    pl.when(odd)(lambda: raw.wait_send())

    @pl.when(sends_f)
    def _():
        for cps in f_cps:
            for cp in cps:
                cp.wait_send()

    @pl.when(even)
    def _():
        for d in ORDER:
            d_cps[d].wait_send()

    @pl.when(odd)
    def _():
        for c in range(C):
            for d in range(1, 4):
                e_cps[c][d].wait_send()
            for d in range(1, 8):
                y_cps[c][d].wait_send()

    for cp in outs:
        cp.wait()


def body(increment, diffusivity, wind, vertical_cov, row_cov, column_cov):
    dma = pltpu.SemaphoreType.DMA
    anyspec = pl.BlockSpec(memory_space=pl.ANY)
    vm = pl.BlockSpec(memory_space=pltpu.VMEM)
    out = pl.pallas_call(
        kernel,
        out_shape=jax.ShapeDtypeStruct((4, NY, NX), F32),
        in_specs=[anyspec, anyspec, vm, vm, vm, vm],
        out_specs=anyspec,
        scratch_shapes=[
            pltpu.VMEM((C, L * ROWS, 128), F32),
            pltpu.VMEM((C, R20, L + 2 * PAD, 128), F32),
            pltpu.VMEM((C, R20, L + 2 * PAD, 128), F32),
            pltpu.VMEM((3, C, ROWS, 128), F32),
            pltpu.VMEM((L, 128), F32),
            pltpu.VMEM((C, L * ROWS, 128), F32),
            pltpu.VMEM((4, C, ROWS, 32, 128), F32),
            pltpu.VMEM((4, C, ROWS, 32, 128), F32),
            pltpu.VMEM((32, C, 32, 128), F32),
            pltpu.VMEM((4, C, ROWS, 32, 128), F32),
            pltpu.VMEM((4, C, ROWS, 32, 128), F32),
            pltpu.VMEM((C, 8, 128, 128), F32),
            pltpu.VMEM((8, C, 128, 128), F32),
            pltpu.VMEM((4, NY, NX), F32),
            pltpu.VMEM((4, NY, NX), F32),
            dma((C,)), dma((C,)), dma((4,)), dma((C,)), dma((C,)), dma,
            dma((2,)), dma((2,)), dma((2,)), dma((2,)), dma, dma,
            dma((C, 4)), dma((C, 4)), dma((C, 4)), dma((C, 4)), dma((C, 8)), dma((C, 8)), dma((32,)), dma((32,)),
            pltpu.SemaphoreType.REGULAR,
        ],
        compiler_params=pltpu.CompilerParams(
            collective_id=0, has_side_effects=True, vmem_limit_bytes=56 * 1024 * 1024
        ),
    )(
        increment.reshape(L * ROWS, NX), diffusivity[0], wind, vertical_cov, row_cov, column_cov
    )
    return out[None]


def solution(mesh):
    in_specs = (P("win", None, "tile", None), P("win", "tile", None), P("win", None), P(), P(), P())
    out_specs = P("win", "tile", None, None)
    return jax.shard_map(body, mesh=mesh, in_specs=in_specs, out_specs=out_specs, check_vma=False)
```

```python
import functools

import jax
import jax.numpy as jnp
from jax import lax
from jax.experimental import pallas as pl
from jax.experimental.pallas import tpu as pltpu
from jax.sharding import PartitionSpec as P

STEPS = 6
L, ROWS, NX = 128, 8, 512
NY = 256
C = NX // 128
H = STEPS
R20 = ROWS + 2 * H
PAD = 8
AHEAD = 2
ORDER = [dz * 8 + dy for dy in (4, 3, 5, 2, 6, 1, 7, 0) for dz in (2, 1, 3, 0) if dz or dy]
MESH = pl.DeviceIdType.MESH
F32, BF16 = jnp.float32, jnp.bfloat16


def split2(v):
    hi = v.astype(BF16)
    lo = (v - hi.astype(F32)).astype(BF16)
    return hi, lo


def kernel(
    inc_ref, dif_ref, wind_ref, vert_ref, row_ref, col_ref, out_ref,
    inb, x, xb, rel, kap, wbuf, fb, mf, me, md, ze, zf, g, rb, zb, ob,
    in_sem, dif_sem, out_sem, loc_e, loc_y, loc_d,
    halo_s, halo_r, rel_s, rel_r, kap_s, kap_r, raw_s, raw_r, f_s, f_r, e_s, e_r, y_s, y_r, d_s, d_r, go_sem,
):
    w = lax.axis_index("win")
    tile = lax.axis_index("tile")
    core = lax.rem(w, 2)
    a = tile // 8
    yy = lax.rem(tile, 8)
    even, odd = core == 0, core == 1
    has_prev, has_next = tile > 0, tile < 31
    sends_f = jnp.logical_and(even, w > 0)
    gets_f = jnp.logical_and(odd, w < 15)

    in_cps = [
        pltpu.make_async_copy(inc_ref.at[:, pl.ds(128 * c, 128)], inb.at[c], in_sem.at[c])
        for c in range(C)
    ]
    for cp in in_cps:
        cp.start()
    dif_cps = [
        pltpu.make_async_copy(dif_ref.at[:, pl.ds(128 * c, 128)], kap.at[1, c], dif_sem.at[c])
        for c in range(C)
    ]
    for cp in dif_cps:
        cp.start()

    bar = pltpu.get_barrier_semaphore()

    def greet(dev):
        pl.semaphore_signal(bar, inc=1, device_id=dev, device_id_type=MESH)

    pl.when(has_prev)(lambda: greet((w, tile - 1)))
    pl.when(has_next)(lambda: greet((w, tile + 1)))

    @pl.when(even)
    def _():
        @pl.loop(1, 32)
        def _(d):
            greet((w, lax.rem(tile + d, 32)))

    @pl.when(odd)
    def _():
        for d in range(1, 4):
            greet((w, lax.rem(a + d, 4) * 8 + yy))
        for d in range(1, 8):
            greet((w, a * 8 + lax.rem(yy + d, 8)))

    sib = w + 1 - 2 * core
    greet((sib, tile))

    @pl.when(gets_f)
    def _():
        for b in range(4):
            greet((w + 1, b * 8 + yy))

    zero8 = jnp.zeros((8, 128), F32)

    @pl.loop(0, R20)
    def _(r):
        for f in (x, xb):
            for c in range(C):
                f[c, r, 0:8, :] = zero8
                f[c, r, PAD + L : PAD + L + 8, :] = zero8

    def clear_rows(first):
        @pl.loop(first, first + H)
        def _(r):
            for f in (x, xb):
                for c in range(C):
                    f[c, r, PAD : PAD + L, :] = jnp.zeros((L, 128), F32)

    pl.when(jnp.logical_not(has_prev))(lambda: clear_rows(0))
    pl.when(jnp.logical_not(has_next))(lambda: clear_rows(H + ROWS))

    wbuf[...] = jnp.transpose(jnp.broadcast_to(wind_ref[...] * 5.0, (128, 128)))
    vert = vert_ref[...]
    vv = jnp.concatenate([vert, vert], axis=1)

    for cp in in_cps:
        cp.wait()
    for c in range(C):
        for y in range(ROWS):
            x[c, H + y, PAD : PAD + L, :] = inb[c, pl.ds(y, L, stride=8), :]
    for cp in dif_cps:
        cp.wait()

    def level_mix(fields, c, dst, scale=None, base=None):
        @pl.loop(0, ROWS // 2)
        def _(pair):
            parts = []
            for i in range(2):
                y = 2 * pair + i
                v = fields[c, H + y, PAD : PAD + L, :]
                if scale is not None:
                    v = v * scale
                if base is not None:
                    v = v - base[c, pl.ds(y, L, stride=8), :]
                parts.append(v)
            hi, lo = split2(jnp.concatenate(parts, axis=1))
            mixed = jnp.dot(vv, jnp.concatenate([hi, lo], axis=0), preferred_element_type=F32)
            for i in range(2):
                if dst is md:
                    at = pl.ds(pl.multiple_of(8 * pair, 8) + 4 * i, 4)
                    for t in range(32):
                        dst[t, c, at, :] = mixed[4 * t : 4 * t + 4, 128 * i : 128 * i + 128]
                    continue
                for b in range(4):
                    dst[b, c, 2 * pair + i] = mixed[32 * b : 32 * b + 32, 128 * i : 128 * i + 128]

    @pl.when(sends_f)
    def _():
        for c in range(C):
            level_mix(x, c, mf)

    peers = jnp.where(even, 32, 11) + has_prev.astype(jnp.int32) + has_next.astype(jnp.int32) + jnp.where(sends_f, 4, 0)
    pl.semaphore_wait(bar, peers)

    def remote(src, dst, ss, rs, dev):
        return pltpu.make_async_remote_copy(
            src_ref=src, dst_ref=dst, send_sem=ss, recv_sem=rs, device_id=dev, device_id_type=MESH
        )

    raw = pltpu.make_async_remote_copy(
        src_ref=inb, dst_ref=fb, send_sem=raw_s, recv_sem=raw_r,
        device_id=(sib, tile), device_id_type=MESH,
    )

    pl.when(odd)(lambda: raw.start())

    f_cps = [
        [
            remote(
                mf.at[lax.rem(a + d, 4), c], zf.at[a, c], f_s.at[c, d], f_r.at[c, d],
                (lax.rem(w + 15, 16), lax.rem(a + d, 4) * 8 + yy),
            )
            for d in range(4)
        ]
        for c in range(C)
    ]

    @pl.when(sends_f)
    def _():
        for cps in f_cps:
            for cp in cps:
                cp.start()


    zs = pl.ds(PAD, L)
    def starts(cps):
        for cp in cps:
            cp.start()

    parts = ((0, 2), (2, 1), (3, 1))

    def halo(way, part, dev, via=None):
        first = (H, ROWS)[way]
        cs = pl.ds(*parts[part])
        return remote(
            x.at[cs, pl.ds(first, H), zs],
            x.at[cs, pl.ds((H + ROWS, 0)[way], H), zs] if via is None else rel.at[pl.ds(part - 1, 1)],
            halo_s.at[way, part], halo_r.at[way, part] if via is None else rel_r.at[part - 1],
            (w, dev if via is None else via),
        )

    ups = [halo(0, n, tile - 1) for n in range(3)]
    downs = [halo(1, n, tile + 1) for n in range(3)]
    ups_via = [halo(0, n, None, tile - 8) for n in (1, 2)]
    downs_via = [halo(1, n, None, tile + 8) for n in (1, 2)]
    at_start, at_end = yy == 0, yy == 7

    def passed(way, part, dev):
        return remote(
            rel.at[pl.ds(part - 1, 1)], x.at[pl.ds(*parts[part]), pl.ds((H + ROWS, 0)[way], H), zs],
            rel_s.at[part - 1], halo_r.at[way, part], (w, dev),
        )

    pass_up = [passed(0, n, tile + 7) for n in (1, 2)]
    pass_down = [passed(1, n, tile - 7) for n in (1, 2)]
    passes_up = jnp.logical_and(at_start, a < 3)
    passes_down = jnp.logical_and(at_end, a > 0)
    kup = remote(kap.at[1], kap.at[2], kap_s.at[0], kap_r.at[0], (w, tile - 1))
    kdown = remote(kap.at[1], kap.at[0], kap_s.at[1], kap_r.at[1], (w, tile + 1))

    @pl.when(has_prev)
    def _():
        kup.start()
        pl.when(at_start)(lambda: starts(ups_via))
        pl.when(jnp.logical_not(at_start))(lambda: starts(ups[1:]))
        ups[0].start()

    @pl.when(has_next)
    def _():
        kdown.start()
        pl.when(at_end)(lambda: starts(downs_via))
        pl.when(jnp.logical_not(at_end))(lambda: starts(downs[1:]))
        downs[0].start()

    @pl.when(w == 15)
    def _():
        @pl.loop(0, 4)
        def _(i):
            for c in range(C):
                zf[i, c] = jnp.zeros((ROWS, 32, 128), F32)

    @pl.when(passes_up)
    def _():
        for got, on in zip(ups_via, pass_up):
            got.wait_recv()
            on.start()

    @pl.when(passes_down)
    def _():
        for got, on in zip(downs_via, pass_down):
            got.wait_recv()
            on.start()

    @pl.when(has_prev)
    def _():
        kup.wait_send()
        kdown.wait_recv()
        for cp in downs:
            cp.wait_recv()

    @pl.when(has_next)
    def _():
        kdown.wait_send()
        kup.wait_recv()
        for cp in ups:
            cp.wait_recv()

    @pl.when(has_prev)
    def _():
        for cp in ups:
            cp.wait_send()

    @pl.when(has_next)
    def _():
        for cp in downs:
            cp.wait_send()


    lane = lax.broadcasted_iota(jnp.int32, (8, 128), 1)
    first_lane, last_lane = lane == 0, lane == 127
    low = jnp.where(has_prev, 0, H)
    high = jnp.where(has_next, R20, H + ROWS)

    def step(s, src, dst):
        @pl.loop(jnp.maximum(low, s + 1), jnp.minimum(high, R20 - 1 - s))
        def _(r):
            kr = r + 2
            kt, ks = kr // 8, lax.rem(kr, 8)
            kb = [jnp.broadcast_to(kap[kt, c, pl.ds(ks, 1), :] * 10.0, (8, 128)) for c in range(C)]
            ab = [8.0 - 4.0 * k for k in kb]
            for zt in range(L // 8):
                z0 = PAD + 8 * zt
                wz = wbuf[8 * zt : 8 * zt + 8, :]
                cs = [src[c, r, z0 : z0 + 8, :] for c in range(C)]
                rr = [pltpu.roll(v, 1, 1) for v in cs]
                rl = [pltpu.roll(v, 127, 1) for v in cs]
                for c in range(C):
                    west = jnp.where(first_lane, rr[(c + C - 1) % C], rr[c])
                    east = jnp.where(last_lane, rl[(c + 1) % C], rl[c])
                    north = src[c, r + 1, z0 : z0 + 8, :]
                    south = src[c, r - 1, z0 : z0 + 8, :]
                    vert_sum = src[c, r, z0 + 1 : z0 + 9, :] + src[c, r, z0 - 1 : z0 + 7, :]
                    dst[c, r, z0 : z0 + 8, :] = (
                        (vert_sum + ab[c] * cs[c])
                        + kb[c] * ((north + south) + (east + west))
                        + wz * (south - north)
                    )

    @pl.loop(0, STEPS // 2)
    def _(h):
        step(2 * h, x, xb)
        step(2 * h + 1, xb, x)

    d_cps = {}
    for d in ORDER:
        dz, dy = d // 8, d % 8
        t = lax.rem(a + dz, 4) * 8 + lax.rem(yy + dy, 8)
        d_cps[d] = remote(
            md.at[t], rb.at[yy, :, pl.ds(pl.multiple_of(32 * a, 32), 32)], d_s.at[d], d_r.at[d], (w, t)
        )
    d_loc = pltpu.make_async_copy(md.at[tile], rb.at[yy, :, pl.ds(pl.multiple_of(32 * a, 32), 32)], loc_d)

    @pl.when(even)
    def _():
        raw.wait_recv()
        for c in range(C):
            level_mix(x, c, md, 1e-6, fb)
        for d in ORDER:
            d_cps[d].start()
        d_loc.start()
        d_loc.wait()

    e_cps = [[None] * 4 for _ in range(C)]
    e_loc = []
    y_cps = [[None] * 8 for _ in range(C)]
    y_loc = []
    for c in range(C):
        for d in (1, 3, 2):
            b = lax.rem(a + d, 4)
            e_cps[c][d] = remote(me.at[b, c], ze.at[a, c], e_s.at[c, d], e_r.at[c, d], (w, b * 8 + yy))
        e_loc.append(pltpu.make_async_copy(me.at[a, c], ze.at[a, c], loc_e.at[c]))
        for d in (1, 7, 2, 6, 3, 5, 4):
            t = lax.rem(yy + d, 8)
            y_cps[c][d] = remote(g.at[c, t], rb.at[yy, c], y_s.at[c, d], y_r.at[c, d], (w, a * 8 + t))
        y_loc.append(pltpu.make_async_copy(g.at[c, yy], rb.at[yy, c], loc_y.at[c]))

    def send_levels(c):
        level_mix(x, c, me, 1e-6)
        if c >= AHEAD:
            for d in (1, 3, 2):
                e_cps[c - AHEAD][d].wait_recv()
        for d in (1, 3, 2):
            e_cps[c][d].start()
        e_loc[c].start()

    def send_rows(c):
        @pl.loop(0, 4)
        def _(i):
            for y in range(ROWS):
                for t in range(4):
                    v = ze[i, c, y, 8 * t : 8 * t + 8, :] - zf[i, c, y, 8 * t : 8 * t + 8, :]
                    at = pl.ds(pl.multiple_of(i * 32, 32) + 4 * y, 4)
                    g[c, 2 * t, at, :] = v[0:4]
                    g[c, 2 * t + 1, at, :] = v[4:8]

        for d in (4, 3, 5, 2, 6, 1, 7):
            y_cps[c][d].start()
        y_loc[c].start()

    @pl.when(odd)
    def _():
        for c in range(AHEAD):
            send_levels(c)
        for c in range(C):
            if c + AHEAD < C:
                send_levels(c + AHEAD)
            else:
                for d in (1, 3, 2):
                    e_cps[c][d].wait_recv()
            e_loc[c].wait()

            @pl.when(gets_f)
            def _(c=c):
                for cp in f_cps[c]:
                    cp.wait_recv()

            send_rows(c)
        for c in range(C):
            y_loc[c].wait()

    for d in (0, 4, 3, 5, 2, 6, 1, 7):
        src = lax.rem(yy + 8 - d, 8)

        @pl.when(even)
        def _(d=d):
            for dz in range(4):
                if dz or d:
                    d_cps[dz * 8 + d].wait_recv()

        if d:

            @pl.when(odd)
            def _(d=d):
                for c in range(C):
                    y_cps[c][d].wait_recv()

        total = None
        for c in range(C):
            v = jnp.concatenate([rb[src, c, pl.ds(z, 32, stride=4), :] for z in range(4)], axis=0)
            hi, lo = split2(v)
            cm = col_ref[128 * c : 128 * c + 128, :]
            part = jnp.dot(hi, cm, preferred_element_type=F32) + jnp.dot(lo, cm, preferred_element_type=F32)
            total = part if total is None else total + part
        for z in range(4):
            for i in range(4):
                k = z * 32 + i * 8
                zb[z, pl.ds(pl.multiple_of(64 * i + 8 * src, 8), 8), :] = total[k : k + 8]

    outs = []
    for z in range(4):
        hi, lo = split2(zb[z])
        rm = row_ref[...]
        ob[z] = jnp.dot(rm, hi, preferred_element_type=F32) + jnp.dot(rm, lo, preferred_element_type=F32)
        cp = pltpu.make_async_copy(ob.at[z], out_ref.at[z], out_sem.at[z])
        cp.start()
        outs.append(cp)

    pl.when(odd)(lambda: raw.wait_send())

    @pl.when(sends_f)
    def _():
        for cps in f_cps:
            for cp in cps:
                cp.wait_send()

    @pl.when(even)
    def _():
        for d in ORDER:
            d_cps[d].wait_send()

    @pl.when(odd)
    def _():
        for c in range(C):
            for d in range(1, 4):
                e_cps[c][d].wait_send()
            for d in range(1, 8):
                y_cps[c][d].wait_send()

    @pl.when(passes_up)
    def _():
        for cp in pass_up:
            cp.wait_send()

    @pl.when(passes_down)
    def _():
        for cp in pass_down:
            cp.wait_send()

    for cp in outs:
        cp.wait()


def body(increment, diffusivity, wind, vertical_cov, row_cov, column_cov):
    dma = pltpu.SemaphoreType.DMA
    anyspec = pl.BlockSpec(memory_space=pl.ANY)
    vm = pl.BlockSpec(memory_space=pltpu.VMEM)
    out = pl.pallas_call(
        kernel,
        out_shape=jax.ShapeDtypeStruct((4, NY, NX), F32),
        in_specs=[anyspec, anyspec, vm, vm, vm, vm],
        out_specs=anyspec,
        scratch_shapes=[
            pltpu.VMEM((C, L * ROWS, 128), F32),
            pltpu.VMEM((C, R20, L + 2 * PAD, 128), F32),
            pltpu.VMEM((C, R20, L + 2 * PAD, 128), F32),
            pltpu.VMEM((C // 2, H, L, 128), F32),
            pltpu.VMEM((3, C, ROWS, 128), F32),
            pltpu.VMEM((L, 128), F32),
            pltpu.VMEM((C, L * ROWS, 128), F32),
            pltpu.VMEM((4, C, ROWS, 32, 128), F32),
            pltpu.VMEM((4, C, ROWS, 32, 128), F32),
            pltpu.VMEM((32, C, 32, 128), F32),
            pltpu.VMEM((4, C, ROWS, 32, 128), F32),
            pltpu.VMEM((4, C, ROWS, 32, 128), F32),
            pltpu.VMEM((C, 8, 128, 128), F32),
            pltpu.VMEM((8, C, 128, 128), F32),
            pltpu.VMEM((4, NY, NX), F32),
            pltpu.VMEM((4, NY, NX), F32),
            dma((C,)), dma((C,)), dma((4,)), dma((C,)), dma((C,)), dma,
            dma((2, 3)), dma((2, 3)), dma((2,)), dma((2,)), dma((2,)), dma((2,)), dma, dma,
            dma((C, 4)), dma((C, 4)), dma((C, 4)), dma((C, 4)), dma((C, 8)), dma((C, 8)), dma((32,)), dma((32,)),
            pltpu.SemaphoreType.REGULAR,
        ],
        compiler_params=pltpu.CompilerParams(
            collective_id=0, has_side_effects=True, vmem_limit_bytes=56 * 1024 * 1024
        ),
    )(
        increment.reshape(L * ROWS, NX), diffusivity[0], wind, vertical_cov, row_cov, column_cov
    )
    return out[None]


def solution(mesh):
    in_specs = (P("win", None, "tile", None), P("win", "tile", None), P("win", None), P(), P(), P())
    out_specs = P("win", "tile", None, None)
    return jax.shard_map(body, mesh=mesh, in_specs=in_specs, out_specs=out_specs, check_vma=False)
```
